128 devices in a mesh: fsdp: 64 (over z, x, y), rep: 2 (over core).
Axes of the slice: x: 4, y: 4, z: 4, core: 2. Of those that a mesh axis runs over, the one named last changes fastest.
Arguments:
- grad_parts: bfloat16 [2, 128, 1024, 1024], P('rep', None, 'fsdp'), may hold values from -6 to 6
- owner_of: int32 [128], replicated, may hold values from 0 to 127, each once
- left_stats: float32 [128, 1024, 1024], P(('fsdp', 'rep')), may hold values from -4 to 4
- right_stats: float32 [128, 1024, 1024], P(('fsdp', 'rep')), may hold values from -4 to 4
- left_root: bfloat16 [128, 1024, 1024], P(('fsdp', 'rep')), may hold values from -0.1875 to 0.1875
- right_root: bfloat16 [128, 1024, 1024], P(('fsdp', 'rep')), may hold values from -0.1875 to 0.1875
Outputs:
- new_left: float32 [128, 1024, 1024], P(('fsdp', 'rep'))
- new_right: float32 [128, 1024, 1024], P(('fsdp', 'rep'))
- direction: bfloat16 [128, 1024, 1024], P(None, ('fsdp', 'rep'))
The draws below stay inside these ranges and needn't reach their ends.
Inputs may be any that keep to these rules, and one draw needn't show every extreme that they name: owner_of is a permutation: every owner slot holds exactly one block.
All inputs are finite; a program needn't handle non-finite values.
Results may differ from the reference program's by a relative error of at most 0.0059.
Values may be sent and summed in bfloat16 or wider, within the bound.
A program may use at most 128 MiB of HBM per device.

```python
import jax
import jax.numpy as jnp
from jax import lax

BS = 1024
BLOCKS = 128
REPLICAS = 2


def block_levels(key, shape, cuts, least, high):
    level = 1.0
    for dim, parts in cuts:
        heights = jax.random.uniform(jax.random.fold_in(jax.random.fold_in(key, 6), dim), (parts,), jnp.float32, least / len(cuts), high / len(cuts))
        level = level * jnp.repeat(jnp.exp(heights), shape[dim] // parts).reshape((-1,) + (1,) * (len(shape) - 1 - dim))
    return level


def scatter_about(rng, shape, spread, reach, cuts=(), held_as=jnp.bfloat16):
    array = spread * jax.random.normal(rng, shape, jnp.float32)
    if cuts:
        array = array * block_levels(rng, shape, cuts, -0.22, 0.18)
    return jnp.clip(array, -reach, reach).astype(held_as)


def setup_inputs(seed: int = 0) -> dict:
    splits = jax.random.split(jax.random.key(seed), 7)
    return {
        "grad_parts": scatter_about(splits[0], (REPLICAS, BLOCKS, BS, BS), 1.0, 6.0, ((0, 2), (2, 64))),
        "owner_of": jax.random.permutation(splits[1], BLOCKS).astype(jnp.int32),
        "left_stats": scatter_about(splits[2], (BLOCKS, BS, BS), 0.5, 4.0, ((0, 128),), jnp.float32),
        "right_stats": scatter_about(splits[3], (BLOCKS, BS, BS), 0.5, 4.0, ((0, 128),), jnp.float32),
        "left_root": scatter_about(splits[4], (BLOCKS, BS, BS), BS ** -0.5, 0.1875, ((0, 128),)),
        "right_root": scatter_about(splits[5], (BLOCKS, BS, BS), BS ** -0.5, 0.1875, ((0, 128),)),
    }


def reference(grad_parts, owner_of, left_stats, right_stats, left_root, right_root):
    by_owner = jnp.zeros_like(owner_of).at[owner_of].set(jnp.arange(BLOCKS, dtype=jnp.int32))
    highest = lax.Precision.HIGHEST

    def owner_update(slot):
        block_index = by_owner[slot]
        summed = jnp.sum(grad_parts[:, block_index].astype(jnp.float32), axis=0)
        left_new = left_stats[slot] + jnp.dot(summed, summed.T, precision=highest) / BS
        right_new = right_stats[slot] + jnp.dot(summed.T, summed, precision=highest) / BS
        rounded = summed.astype(jnp.bfloat16)
        applied = jnp.dot(left_root[slot], rounded, preferred_element_type=jnp.float32).astype(jnp.bfloat16)
        direction = jnp.dot(applied, right_root[slot], preferred_element_type=jnp.float32).astype(jnp.bfloat16)
        return left_new, right_new, direction

    new_left, new_right, by_slot = lax.map(owner_update, jnp.arange(BLOCKS, dtype=jnp.int32))
    return new_left, new_right, by_slot[owner_of]
```

```python
import jax
import jax.numpy as jnp
from jax import lax
from jax.experimental import pallas as pl
from jax.experimental.pallas import tpu as pltpu
from jax.sharding import PartitionSpec as P

MESH = pl.DeviceIdType.MESH
CHIPS = 64
BS = 1024
BLOCKS = 128
ROWS = BS // CHIPS
HALF = ROWS // 2
CHUNK = 8
LEAP = 21
BF16 = jnp.bfloat16
F32 = jnp.float32


def partner_chip(me, step):
    o = lax.rem(step * LEAP, CHIPS)
    z = lax.rem(lax.div(me, 16) + lax.div(o, 16), 4)
    x = lax.rem(lax.div(me, 4) + lax.div(o, 4), 4)
    y = lax.rem(me + o, 4)
    return z * 16 + x * 4 + y


def kernel(
    by_owner, owner_of, grad_hbm, lstat_hbm, rstat_hbm, lroot_hbm, rroot_hbm,
    new_left, new_right, direction,
    grad, stage, partner_part, summed, gathered, lroot, lperm, rroot, outgoing, returned,
    load_sem, swap_send, swap_recv, fwd_send, fwd_recv, back_send, back_recv,
):
    f = lax.axis_index("fsdp")
    r = lax.axis_index("rep")
    other = 1 - r
    me = 2 * f + r

    load_grad = pltpu.make_async_copy(grad_hbm.at[0], grad, load_sem.at[0])
    load_grad.start()

    barrier = pltpu.get_barrier_semaphore()

    @pl.loop(1, 2 * CHIPS)
    def _(k):
        d = lax.rem(me + k, 2 * CHIPS)
        pl.semaphore_signal(
            barrier, inc=1, device_id=(lax.div(d, 2), lax.rem(d, 2)), device_id_type=MESH
        )

    loads = [
        pltpu.make_async_copy(lroot_hbm.at[0], lroot, load_sem.at[1]),
        pltpu.make_async_copy(rroot_hbm.at[0], rroot, load_sem.at[2]),
        pltpu.make_async_copy(lstat_hbm.at[0], new_left.at[0], load_sem.at[3]),
        pltpu.make_async_copy(rstat_hbm.at[0], new_right.at[0], load_sem.at[4]),
    ]
    for load in loads:
        load.start()
    load_grad.wait()
    pl.semaphore_wait(barrier, 2 * CHIPS - 1)

    def swap(c):
        part = pl.ds(c * CHUNK, CHUNK)
        return pltpu.make_async_remote_copy(
            stage.at[part], partner_part.at[part], swap_send.at[c], swap_recv.at[c],
            device_id=(f, other), device_id_type=MESH,
        )

    @pl.loop(0, CHIPS // CHUNK)
    def _(c):
        @pl.loop(0, CHUNK)
        def _(j):
            i = c * CHUNK + j
            stage[i] = grad[by_owner[2 * partner_chip(f, i) + other]]

        swap(c).start()

    @pl.loop(0, CHIPS // CHUNK)
    def _(c):
        swap(c).wait_recv()

        @pl.loop(0, CHUNK)
        def _(j):
            i = c * CHUNK + j
            to = partner_chip(f, i)
            mine = grad[by_owner[2 * to + r]].astype(F32)
            summed[i] = (mine + partner_part[i].astype(F32)).astype(BF16)

            @pl.when(i > 0)
            def _():
                pltpu.make_async_remote_copy(
                    summed.at[i], gathered.at[f], fwd_send, fwd_recv,
                    device_id=(to, r), device_id_type=MESH,
                ).start()

    gathered[f] = summed[0]
    for load in loads:
        load.wait()

    @pl.loop(0, CHIPS)
    def _(i):
        lperm[i] = lroot[pl.ds(pl.multiple_of(partner_chip(f, i) * ROWS, ROWS), ROWS), :]

    rest = pl.ds(0, CHIPS - 1)
    pltpu.make_async_copy(gathered.at[rest], gathered.at[rest], fwd_recv).wait()

    @pl.loop(0, CHIPS // CHUNK)
    def _(c):
        part = lperm[pl.ds(c * CHUNK, CHUNK)].reshape(CHUNK * ROWS, BS)
        whole = gathered[...].reshape(BS, BS)
        applied = jnp.dot(part, whole, preferred_element_type=F32).astype(BF16)
        done = jnp.dot(applied, rroot[...], preferred_element_type=F32)
        outgoing[pl.ds(c * 2 * CHUNK, 2 * CHUNK)] = done.reshape(2 * CHUNK, HALF, BS).astype(BF16)

        @pl.loop(0, 2 * CHUNK)
        def _(j):
            h = c * 2 * CHUNK + j
            to = partner_chip(f, lax.div(h, 2))
            core = lax.rem(h, 2)

            @pl.when(2 * to + core != me)
            def _():
                pltpu.make_async_remote_copy(
                    outgoing.at[h], returned.at[me], back_send, back_recv,
                    device_id=(to, core), device_id_type=MESH,
                ).start()

    returned[me] = outgoing[r]

    @pl.loop(0, 4)
    def _(c):
        rows = pl.ds(pl.multiple_of(c * 256, 256), 256)
        whole = gathered[...].reshape(BS, BS)
        part = gathered[pl.ds(c * 16, 16)].reshape(256, BS)
        gram = lax.dot_general(part, whole, (((1,), (1,)), ((), ())), preferred_element_type=F32)
        new_left[0, rows, :] += gram * (1.0 / BS)

    @pl.loop(0, 4)
    def _(c):
        rows = pl.ds(pl.multiple_of(c * 256, 256), 256)
        whole = gathered[...].reshape(BS, BS)
        part = gathered[:, :, rows].reshape(BS, 256)
        gram = lax.dot_general(part, whole, (((0,), (0,)), ((), ())), preferred_element_type=F32)
        new_right[0, rows, :] += gram * (1.0 / BS)

    @pl.loop(0, CHIPS // CHUNK)
    def _(c):
        swap(c).wait_send()

    pltpu.make_async_copy(gathered.at[rest], gathered.at[rest], fwd_send).wait()
    all_but_me = pl.ds(0, BLOCKS - 1)
    pltpu.make_async_copy(returned.at[all_but_me], returned.at[all_but_me], back_send).wait()
    pltpu.make_async_copy(returned.at[all_but_me], returned.at[all_but_me], back_recv).wait()

    @pl.loop(0, BLOCKS)
    def _(b):
        direction[b] = returned[owner_of[b]]


def body(grad_parts, owner_of, left_stats, right_stats, left_root, right_root):
    blocks = jnp.arange(BLOCKS, dtype=jnp.int32)
    by_owner = jnp.sum(
        jnp.where(owner_of[None, :] == blocks[:, None], blocks[None, :], 0), axis=1, dtype=jnp.int32
    )
    smem = pl.BlockSpec(memory_space=pltpu.SMEM)
    anywhere = pl.BlockSpec(memory_space=pl.ANY)
    vmem = pl.BlockSpec(memory_space=pltpu.VMEM)
    return pl.pallas_call(
        kernel,
        out_shape=(
            jax.ShapeDtypeStruct((1, BS, BS), F32),
            jax.ShapeDtypeStruct((1, BS, BS), F32),
            jax.ShapeDtypeStruct((BLOCKS, HALF, BS), BF16),
        ),
        in_specs=[smem, smem] + [anywhere] * 5,
        out_specs=(vmem, vmem, vmem),
        scratch_shapes=[
            pltpu.VMEM((BLOCKS, ROWS, BS), BF16),
            pltpu.VMEM((CHIPS, ROWS, BS), BF16),
            pltpu.VMEM((CHIPS, ROWS, BS), BF16),
            pltpu.VMEM((CHIPS, ROWS, BS), BF16),
            pltpu.VMEM((CHIPS, ROWS, BS), BF16),
            pltpu.VMEM((BS, BS), BF16),
            pltpu.VMEM((CHIPS, ROWS, BS), BF16),
            pltpu.VMEM((BS, BS), BF16),
            pltpu.VMEM((BLOCKS, HALF, BS), BF16),
            pltpu.VMEM((BLOCKS, HALF, BS), BF16),
            pltpu.SemaphoreType.DMA((5,)),
            pltpu.SemaphoreType.DMA((CHIPS // CHUNK,)),
            pltpu.SemaphoreType.DMA((CHIPS // CHUNK,)),
            pltpu.SemaphoreType.DMA,
            pltpu.SemaphoreType.DMA,
            pltpu.SemaphoreType.DMA,
            pltpu.SemaphoreType.DMA,
        ],
        compiler_params=pltpu.CompilerParams(
            collective_id=0, has_side_effects=True, vmem_limit_bytes=56 * 2**20
        ),
        cost_estimate=pl.CostEstimate(
            flops=8 * BS**3, bytes_accessed=26 * 2**20, transcendentals=0
        ),
        name="shampoo_step",
    )(by_owner, owner_of, grad_parts, left_stats, right_stats, left_root, right_root)


def solution(mesh):
    placed = (
        P("rep", None, "fsdp", None),
        P(),
        P(("fsdp", "rep"), None, None),
        P(("fsdp", "rep"), None, None),
        P(("fsdp", "rep"), None, None),
        P(("fsdp", "rep"), None, None),
    )
    return jax.shard_map(
        body,
        mesh=mesh,
        in_specs=placed,
        out_specs=(
            P(("fsdp", "rep"), None, None),
            P(("fsdp", "rep"), None, None),
            P(None, ("fsdp", "rep"), None),
        ),
        check_vma=False,
    )
```

```python
import jax
import jax.numpy as jnp
from jax import lax
from jax.experimental import pallas as pl
from jax.experimental.pallas import tpu as pltpu
from jax.sharding import PartitionSpec as P

MESH = pl.DeviceIdType.MESH
CHIPS = 64
BS = 1024
BLOCKS = 128
ROWS = BS // CHIPS
HALF = ROWS // 2
CHUNK = 8
LEAP = 27
BF16 = jnp.bfloat16
F32 = jnp.float32


def partner_chip(me, step):
    o = lax.rem(step * LEAP, CHIPS)
    z = lax.rem(lax.div(me, 16) + lax.div(o, 16), 4)
    x = lax.rem(lax.div(me, 4) + lax.div(o, 4), 4)
    y = lax.rem(me + o, 4)
    return z * 16 + x * 4 + y


def kernel(
    owner_of, grad_hbm, lstat_hbm, rstat_hbm, lroot_hbm, rroot_hbm,
    new_left, new_right, returned,
    grad, stage, partner_part, summed, gathered, lroot, lperm, rroot, outgoing,
    by_owner_v, by_owner,
    load_sem, swap_send, swap_recv, fwd_send, fwd_recv, back_send, back_recv,
):
    f = lax.axis_index("fsdp")
    r = lax.axis_index("rep")
    other = 1 - r
    me = 2 * f + r

    load_grad = pltpu.make_async_copy(grad_hbm.at[0], grad, load_sem.at[0])
    load_grad.start()

    barrier = pltpu.get_barrier_semaphore()

    @pl.loop(1, 2 * CHIPS)
    def _(k):
        d = lax.rem(me + k, 2 * CHIPS)
        pl.semaphore_signal(
            barrier, inc=1, device_id=(lax.div(d, 2), lax.rem(d, 2)), device_id_type=MESH
        )

    loads = [
        pltpu.make_async_copy(lroot_hbm.at[0], lroot, load_sem.at[1]),
        pltpu.make_async_copy(rroot_hbm.at[0], rroot, load_sem.at[2]),
        pltpu.make_async_copy(lstat_hbm.at[0], new_left.at[0], load_sem.at[3]),
        pltpu.make_async_copy(rstat_hbm.at[0], new_right.at[0], load_sem.at[4]),
    ]
    for load in loads:
        load.start()
    slot = lax.broadcasted_iota(jnp.int32, (BLOCKS, BLOCKS), 0)
    block = lax.broadcasted_iota(jnp.int32, (BLOCKS, BLOCKS), 1)
    held = jnp.where(jnp.broadcast_to(owner_of[...], (BLOCKS, BLOCKS)) == slot, block, 0)
    by_owner_v[...] = jnp.max(held.T, axis=0, keepdims=True)
    to_smem = pltpu.make_async_copy(by_owner_v, by_owner, load_sem.at[5])
    to_smem.start()
    to_smem.wait()
    load_grad.wait()
    pl.semaphore_wait(barrier, 2 * CHIPS - 1)

    def swap(c):
        part = pl.ds(c * CHUNK, CHUNK)
        return pltpu.make_async_remote_copy(
            stage.at[part], partner_part.at[part], swap_send.at[c], swap_recv.at[c],
            device_id=(f, other), device_id_type=MESH,
        )

    @pl.loop(0, CHIPS // CHUNK)
    def _(c):
        @pl.loop(0, CHUNK)
        def _(j):
            i = c * CHUNK + j
            stage[i] = grad[by_owner[0, 2 * partner_chip(f, i) + other]]

        swap(c).start()

    @pl.loop(0, CHIPS // CHUNK)
    def _(c):
        swap(c).wait_recv()

        @pl.loop(0, CHUNK)
        def _(j):
            i = c * CHUNK + j
            to = partner_chip(f, i)
            mine = grad[by_owner[0, 2 * to + r]].astype(F32)
            summed[i] = (mine + partner_part[i].astype(F32)).astype(BF16)

            @pl.when(i > 0)
            def _():
                pltpu.make_async_remote_copy(
                    summed.at[i], gathered.at[f], fwd_send, fwd_recv,
                    device_id=(to, r), device_id_type=MESH,
                ).start()

    gathered[f] = summed[0]
    for load in loads:
        load.wait()

    @pl.loop(0, CHIPS)
    def _(i):
        lperm[i] = lroot[pl.ds(pl.multiple_of(partner_chip(f, i) * ROWS, ROWS), ROWS), :]

    rest = pl.ds(0, CHIPS - 1)
    pltpu.make_async_copy(gathered.at[rest], gathered.at[rest], fwd_recv).wait()

    @pl.loop(0, CHIPS // CHUNK)
    def _(c):
        part = lperm[pl.ds(c * CHUNK, CHUNK)].reshape(CHUNK * ROWS, BS)
        whole = gathered[...].reshape(BS, BS)
        applied = jnp.dot(part, whole, preferred_element_type=F32).astype(BF16)
        done = jnp.dot(applied, rroot[...], preferred_element_type=F32)
        outgoing[pl.ds(c * 2 * CHUNK, 2 * CHUNK)] = done.reshape(2 * CHUNK, HALF, BS).astype(BF16)

        @pl.loop(0, 2 * CHUNK)
        def _(j):
            h = c * 2 * CHUNK + j
            to = partner_chip(f, lax.div(h, 2))
            core = lax.rem(h, 2)

            @pl.when(2 * to + core != me)
            def _():
                pltpu.make_async_remote_copy(
                    outgoing.at[h], returned.at[me], back_send, back_recv,
                    device_id=(to, core), device_id_type=MESH,
                ).start()

    returned[me] = outgoing[r]

    @pl.loop(0, 4)
    def _(c):
        rows = pl.ds(pl.multiple_of(c * 256, 256), 256)
        whole = gathered[...].reshape(BS, BS)
        part = gathered[pl.ds(c * 16, 16)].reshape(256, BS)
        gram = lax.dot_general(part, whole, (((1,), (1,)), ((), ())), preferred_element_type=F32)
        new_left[0, rows, :] += gram * (1.0 / BS)

    @pl.loop(0, 4)
    def _(c):
        rows = pl.ds(pl.multiple_of(c * 256, 256), 256)
        whole = gathered[...].reshape(BS, BS)
        part = gathered[:, :, rows].reshape(BS, 256)
        gram = lax.dot_general(part, whole, (((0,), (0,)), ((), ())), preferred_element_type=F32)
        new_right[0, rows, :] += gram * (1.0 / BS)

    @pl.loop(0, CHIPS // CHUNK)
    def _(c):
        swap(c).wait_send()

    pltpu.make_async_copy(gathered.at[rest], gathered.at[rest], fwd_send).wait()
    all_but_me = pl.ds(0, BLOCKS - 1)
    pltpu.make_async_copy(returned.at[all_but_me], returned.at[all_but_me], back_send).wait()
    pltpu.make_async_copy(returned.at[all_but_me], returned.at[all_but_me], back_recv).wait()


def write_out(owner_of, left, right, returned, new_left, new_right, direction, sem):
    writes = [
        pltpu.make_async_copy(left, new_left, sem.at[0]),
        pltpu.make_async_copy(right, new_right, sem.at[1]),
    ]
    for write in writes:
        write.start()

    @pl.loop(0, BLOCKS)
    def _(b):
        pltpu.make_async_copy(returned.at[owner_of[b]], direction.at[b], sem.at[2]).start()

    for write in writes:
        write.wait()
    pltpu.make_async_copy(returned, direction, sem.at[2]).wait()


def body(grad_parts, owner_of, left_stats, right_stats, left_root, right_root):
    anywhere = pl.BlockSpec(memory_space=pl.ANY)
    vmem = pl.BlockSpec(memory_space=pltpu.VMEM)
    smem = pl.BlockSpec(memory_space=pltpu.SMEM)
    left, right, returned = pl.pallas_call(
        kernel,
        out_shape=(
            pltpu.VMEM((1, BS, BS), F32),
            pltpu.VMEM((1, BS, BS), F32),
            pltpu.VMEM((BLOCKS, HALF, BS), BF16),
        ),
        in_specs=[vmem] + [anywhere] * 5,
        out_specs=(vmem, vmem, vmem),
        scratch_shapes=[
            pltpu.VMEM((BLOCKS, ROWS, BS), BF16),
            pltpu.VMEM((CHIPS, ROWS, BS), BF16),
            pltpu.VMEM((CHIPS, ROWS, BS), BF16),
            pltpu.VMEM((CHIPS, ROWS, BS), BF16),
            pltpu.VMEM((CHIPS, ROWS, BS), BF16),
            pltpu.VMEM((BS, BS), BF16),
            pltpu.VMEM((CHIPS, ROWS, BS), BF16),
            pltpu.VMEM((BS, BS), BF16),
            pltpu.VMEM((BLOCKS, HALF, BS), BF16),
            pltpu.VMEM((1, BLOCKS), jnp.int32),
            pltpu.SMEM((1, BLOCKS), jnp.int32),
            pltpu.SemaphoreType.DMA((6,)),
            pltpu.SemaphoreType.DMA((CHIPS // CHUNK,)),
            pltpu.SemaphoreType.DMA((CHIPS // CHUNK,)),
            pltpu.SemaphoreType.DMA,
            pltpu.SemaphoreType.DMA,
            pltpu.SemaphoreType.DMA,
            pltpu.SemaphoreType.DMA,
        ],
        compiler_params=pltpu.CompilerParams(
            collective_id=0, has_side_effects=True, vmem_limit_bytes=52 * 2**20
        ),
        cost_estimate=pl.CostEstimate(
            flops=8 * BS**3, bytes_accessed=16 * 2**20, transcendentals=0
        ),
        name="shampoo_step",
    )(owner_of[None], grad_parts, left_stats, right_stats, left_root, right_root)
    return pl.pallas_call(
        write_out,
        out_shape=(
            jax.ShapeDtypeStruct((1, BS, BS), F32),
            jax.ShapeDtypeStruct((1, BS, BS), F32),
            jax.ShapeDtypeStruct((BLOCKS, HALF, BS), BF16),
        ),
        in_specs=[smem] + [anywhere] * 3,
        out_specs=(anywhere, anywhere, anywhere),
        scratch_shapes=[pltpu.SemaphoreType.DMA((3,))],
        compiler_params=pltpu.CompilerParams(vmem_limit_bytes=2 * 2**20),
        name="write_out",
    )(owner_of, left, right, returned)


def solution(mesh):
    placed = (
        P("rep", None, "fsdp", None),
        P(),
        P(("fsdp", "rep"), None, None),
        P(("fsdp", "rep"), None, None),
        P(("fsdp", "rep"), None, None),
        P(("fsdp", "rep"), None, None),
    )
    return jax.shard_map(
        body,
        mesh=mesh,
        in_specs=placed,
        out_specs=(
            P(("fsdp", "rep"), None, None),
            P(("fsdp", "rep"), None, None),
            P(None, ("fsdp", "rep"), None),
        ),
        check_vma=False,
    )
```

```python
import jax
import jax.numpy as jnp
from jax import lax
from jax.experimental import pallas as pl
from jax.experimental.pallas import tpu as pltpu
from jax.sharding import PartitionSpec as P

MESH = pl.DeviceIdType.MESH
CHIPS = 64
BS = 1024
BLOCKS = 128
ROWS = BS // CHIPS
HALF = ROWS // 2
CHUNK = 8
LEAP = 27
BF16 = jnp.bfloat16
F32 = jnp.float32


def partner_chip(me, step):
    o = lax.rem(step * LEAP, CHIPS)
    z = lax.rem(lax.div(me, 16) + lax.div(o, 16), 4)
    x = lax.rem(lax.div(me, 4) + lax.div(o, 4), 4)
    y = lax.rem(me + o, 4)
    return z * 16 + x * 4 + y


def kernel(
    owner_of, grad_hbm, lstat_hbm, rstat_hbm, lroot_hbm, rroot_hbm,
    new_left, new_right, returned,
    grad, stage, partner_part, summed, gathered, lroot, lperm, rroot, outgoing,
    by_owner_v, by_owner,
    load_sem, swap_send, swap_recv, fwd_send, fwd_recv, back_send, back_recv, go,
):
    f = lax.axis_index("fsdp")
    r = lax.axis_index("rep")
    other = 1 - r
    me = 2 * f + r

    load_grad = pltpu.make_async_copy(grad_hbm.at[0], grad, load_sem.at[0])
    load_grad.start()

    barrier = pltpu.get_barrier_semaphore()

    pl.semaphore_signal(barrier, inc=1, device_id=(f, other), device_id_type=MESH)

    @pl.loop(1, CHIPS)
    def _(k):
        pl.semaphore_signal(
            barrier, inc=1, device_id=(lax.rem(f + k, CHIPS), r), device_id_type=MESH
        )

    loads = [
        pltpu.make_async_copy(lroot_hbm.at[0], lroot, load_sem.at[1]),
        pltpu.make_async_copy(rroot_hbm.at[0], rroot, load_sem.at[2]),
        pltpu.make_async_copy(lstat_hbm.at[0], new_left.at[0], load_sem.at[3]),
        pltpu.make_async_copy(rstat_hbm.at[0], new_right.at[0], load_sem.at[4]),
    ]
    slot = lax.broadcasted_iota(jnp.int32, (BLOCKS, BLOCKS), 0)
    block = lax.broadcasted_iota(jnp.int32, (BLOCKS, BLOCKS), 1)
    held = jnp.where(jnp.broadcast_to(owner_of[...], (BLOCKS, BLOCKS)) == slot, block, 0)
    by_owner_v[...] = jnp.max(held.T, axis=0, keepdims=True)
    to_smem = pltpu.make_async_copy(by_owner_v, by_owner, load_sem.at[5])
    to_smem.start()
    to_smem.wait()
    load_grad.wait()
    for load in loads:
        load.start()
    pl.semaphore_wait(barrier, CHIPS)

    def swap(c):
        part = pl.ds(c * CHUNK, CHUNK)
        return pltpu.make_async_remote_copy(
            stage.at[part], partner_part.at[part], swap_send.at[c], swap_recv.at[c],
            device_id=(f, other), device_id_type=MESH,
        )

    @pl.loop(0, CHIPS // CHUNK)
    def _(c):
        @pl.loop(0, CHUNK)
        def _(j):
            i = c * CHUNK + j
            stage[i] = grad[by_owner[0, 2 * partner_chip(f, i) + other]]

        swap(c).start()

    def forward(i, to):
        return pltpu.make_async_remote_copy(
            summed.at[i], gathered.at[f], fwd_send.at[lax.div(i, 32)], fwd_recv,
            device_id=(to, r), device_id_type=MESH,
        )

    @pl.loop(0, CHIPS // CHUNK)
    def _(c):
        swap(c).wait_recv()

        @pl.loop(0, CHUNK)
        def _(j):
            i = c * CHUNK + j
            to = partner_chip(f, i)
            mine = grad[by_owner[0, 2 * to + r]].astype(F32)
            summed[i] = (mine + partner_part[i].astype(F32)).astype(BF16)

            @pl.when(jnp.logical_and(i > 0, r == 0))
            def _():
                forward(i, to).start()

    gathered[f] = summed[0]
    for load in loads:
        load.wait()

    @pl.loop(0, CHIPS)
    def _(i):
        lperm[i] = lroot[pl.ds(pl.multiple_of(partner_chip(f, i) * ROWS, ROWS), ROWS), :]

    rest = pl.ds(0, CHIPS - 1)

    @pl.when(r == 0)
    def _():
        soon = pl.ds(0, 32 - 1)
        pltpu.make_async_copy(gathered.at[soon], gathered.at[soon], fwd_send.at[0]).wait()
        pl.semaphore_signal(go, inc=1, device_id=(f, other), device_id_type=MESH)

    @pl.when(r == 1)
    def _():
        pl.semaphore_wait(go, 1)

        @pl.loop(1, CHIPS)
        def _(i):
            forward(i, partner_chip(f, i)).start()

    pltpu.make_async_copy(gathered.at[rest], gathered.at[rest], fwd_recv).wait()

    @pl.loop(0, CHIPS // CHUNK)
    def _(c):
        part = lperm[pl.ds(c * CHUNK, CHUNK)].reshape(CHUNK * ROWS, BS)
        whole = gathered[...].reshape(BS, BS)
        applied = jnp.dot(part, whole, preferred_element_type=F32).astype(BF16)
        done = jnp.dot(applied, rroot[...], preferred_element_type=F32)
        outgoing[pl.ds(c * 2 * CHUNK, 2 * CHUNK)] = done.reshape(2 * CHUNK, HALF, BS).astype(BF16)

        @pl.loop(0, 2 * CHUNK)
        def _(j):
            h = c * 2 * CHUNK + j
            to = partner_chip(f, lax.div(h, 2))
            core = lax.rem(h, 2)

            @pl.when(2 * to + core != me)
            def _():
                pltpu.make_async_remote_copy(
                    outgoing.at[h], returned.at[me], back_send, back_recv,
                    device_id=(to, core), device_id_type=MESH,
                ).start()

    returned[me] = outgoing[r]

    @pl.loop(0, 4)
    def _(c):
        rows = pl.ds(pl.multiple_of(c * 256, 256), 256)
        whole = gathered[...].reshape(BS, BS)
        part = gathered[pl.ds(c * 16, 16)].reshape(256, BS)
        gram = lax.dot_general(part, whole, (((1,), (1,)), ((), ())), preferred_element_type=F32)
        new_left[0, rows, :] += gram * (1.0 / BS)

    @pl.loop(0, 4)
    def _(c):
        rows = pl.ds(pl.multiple_of(c * 256, 256), 256)
        whole = gathered[...].reshape(BS, BS)
        part = gathered[:, :, rows].reshape(BS, 256)
        gram = lax.dot_general(part, whole, (((0,), (0,)), ((), ())), preferred_element_type=F32)
        new_right[0, rows, :] += gram * (1.0 / BS)

    @pl.loop(0, CHIPS // CHUNK)
    def _(c):
        swap(c).wait_send()

    late = pl.ds(0, 32)
    pltpu.make_async_copy(gathered.at[late], gathered.at[late], fwd_send.at[1]).wait()

    @pl.when(r == 1)
    def _():
        soon = pl.ds(0, 32 - 1)
        pltpu.make_async_copy(gathered.at[soon], gathered.at[soon], fwd_send.at[0]).wait()

    all_but_me = pl.ds(0, BLOCKS - 1)
    pltpu.make_async_copy(returned.at[all_but_me], returned.at[all_but_me], back_send).wait()
    pltpu.make_async_copy(returned.at[all_but_me], returned.at[all_but_me], back_recv).wait()


def write_out(owner_of, left, right, returned, new_left, new_right, direction, sem):
    writes = [
        pltpu.make_async_copy(left, new_left, sem.at[0]),
        pltpu.make_async_copy(right, new_right, sem.at[1]),
    ]
    for write in writes:
        write.start()

    @pl.loop(0, BLOCKS)
    def _(b):
        pltpu.make_async_copy(returned.at[owner_of[b]], direction.at[b], sem.at[2]).start()

    for write in writes:
        write.wait()
    pltpu.make_async_copy(returned, direction, sem.at[2]).wait()


def body(grad_parts, owner_of, left_stats, right_stats, left_root, right_root):
    anywhere = pl.BlockSpec(memory_space=pl.ANY)
    vmem = pl.BlockSpec(memory_space=pltpu.VMEM)
    smem = pl.BlockSpec(memory_space=pltpu.SMEM)
    left, right, returned = pl.pallas_call(
        kernel,
        out_shape=(
            pltpu.VMEM((1, BS, BS), F32),
            pltpu.VMEM((1, BS, BS), F32),
            pltpu.VMEM((BLOCKS, HALF, BS), BF16),
        ),
        in_specs=[vmem] + [anywhere] * 5,
        out_specs=(vmem, vmem, vmem),
        scratch_shapes=[
            pltpu.VMEM((BLOCKS, ROWS, BS), BF16),
            pltpu.VMEM((CHIPS, ROWS, BS), BF16),
            pltpu.VMEM((CHIPS, ROWS, BS), BF16),
            pltpu.VMEM((CHIPS, ROWS, BS), BF16),
            pltpu.VMEM((CHIPS, ROWS, BS), BF16),
            pltpu.VMEM((BS, BS), BF16),
            pltpu.VMEM((CHIPS, ROWS, BS), BF16),
            pltpu.VMEM((BS, BS), BF16),
            pltpu.VMEM((BLOCKS, HALF, BS), BF16),
            pltpu.VMEM((1, BLOCKS), jnp.int32),
            pltpu.SMEM((1, BLOCKS), jnp.int32),
            pltpu.SemaphoreType.DMA((6,)),
            pltpu.SemaphoreType.DMA((CHIPS // CHUNK,)),
            pltpu.SemaphoreType.DMA((CHIPS // CHUNK,)),
            pltpu.SemaphoreType.DMA((2,)),
            pltpu.SemaphoreType.DMA,
            pltpu.SemaphoreType.DMA,
            pltpu.SemaphoreType.DMA,
            pltpu.SemaphoreType.REGULAR,
        ],
        compiler_params=pltpu.CompilerParams(
            collective_id=0, has_side_effects=True, vmem_limit_bytes=52 * 2**20
        ),
        cost_estimate=pl.CostEstimate(
            flops=8 * BS**3, bytes_accessed=16 * 2**20, transcendentals=0
        ),
        name="shampoo_step",
    )(owner_of[None], grad_parts, left_stats, right_stats, left_root, right_root)
    return pl.pallas_call(
        write_out,
        out_shape=(
            jax.ShapeDtypeStruct((1, BS, BS), F32),
            jax.ShapeDtypeStruct((1, BS, BS), F32),
            jax.ShapeDtypeStruct((BLOCKS, HALF, BS), BF16),
        ),
        in_specs=[smem] + [anywhere] * 3,
        out_specs=(anywhere, anywhere, anywhere),
        scratch_shapes=[pltpu.SemaphoreType.DMA((3,))],
        compiler_params=pltpu.CompilerParams(vmem_limit_bytes=2 * 2**20),
        name="write_out",
    )(owner_of, left, right, returned)


def solution(mesh):
    placed = (
        P("rep", None, "fsdp", None),
        P(),
        P(("fsdp", "rep"), None, None),
        P(("fsdp", "rep"), None, None),
        P(("fsdp", "rep"), None, None),
        P(("fsdp", "rep"), None, None),
    )
    return jax.shard_map(
        body,
        mesh=mesh,
        in_specs=placed,
        out_specs=(
            P(("fsdp", "rep"), None, None),
            P(("fsdp", "rep"), None, None),
            P(None, ("fsdp", "rep"), None),
        ),
        check_vma=False,
    )
```

```python
import jax
import jax.numpy as jnp
from jax import lax
from jax.experimental import pallas as pl
from jax.experimental.pallas import tpu as pltpu
from jax.sharding import PartitionSpec as P

MESH = pl.DeviceIdType.MESH
CHIPS = 64
BS = 1024
BLOCKS = 128
ROWS = BS // CHIPS
HALF = ROWS // 2
CHUNK = 8
LGR_CHUNK = 16
LEAP = 53
BF16 = jnp.bfloat16
F32 = jnp.float32


def partner_chip(me, step):
    o = lax.rem(step * LEAP, CHIPS)
    z = lax.rem(lax.div(me, 16) + lax.div(o, 16), 4)
    x = lax.rem(lax.div(me, 4) + lax.div(o, 4), 4)
    y = lax.rem(me + o, 4)
    return z * 16 + x * 4 + y


def source_chip(me, step):
    o = lax.rem(step * LEAP, CHIPS)
    z = lax.rem(lax.div(me, 16) + 4 - lax.div(o, 16), 4)
    x = lax.rem(lax.div(me, 4) + 8 - lax.rem(lax.div(o, 4), 4), 4)
    y = lax.rem(me + 4 - lax.rem(o, 4), 4)
    return z * 16 + x * 4 + y


def kernel(
    owner_hbm, grad_hbm, lstat_hbm, rstat_hbm, lroot_hbm, rroot_hbm,
    new_left, new_right, returned,
    grad, stage, partner_part, summed, gathered, lroot, lperm, rroot, outgoing,
    owner_of, by_owner_v, by_owner,
    load_sem, swap_send, swap_recv, fwd_send, fwd_recv, back_send, back_recv,
):
    f = lax.axis_index("fsdp")
    r = lax.axis_index("rep")
    other = 1 - r
    me = 2 * f + r

    load_owner = pltpu.make_async_copy(owner_hbm, owner_of, load_sem.at[6])
    load_owner.start()
    load_grad = pltpu.make_async_copy(grad_hbm.at[0], grad, load_sem.at[0])
    load_grad.start()

    barrier = pltpu.get_barrier_semaphore()

    pl.semaphore_signal(barrier, inc=1, device_id=(f, other), device_id_type=MESH)

    @pl.loop(1, CHIPS)
    def _(k):
        pl.semaphore_signal(
            barrier, inc=1, device_id=(source_chip(f, k), lax.rem(k, 2)), device_id_type=MESH
        )

    loads = [
        pltpu.make_async_copy(lroot_hbm.at[0], lroot, load_sem.at[1]),
        pltpu.make_async_copy(rroot_hbm.at[0], rroot, load_sem.at[2]),
        pltpu.make_async_copy(lstat_hbm.at[0], new_left.at[0], load_sem.at[3]),
        pltpu.make_async_copy(rstat_hbm.at[0], new_right.at[0], load_sem.at[4]),
    ]
    load_owner.wait()
    slot = lax.broadcasted_iota(jnp.int32, (BLOCKS, BLOCKS), 0)
    block = lax.broadcasted_iota(jnp.int32, (BLOCKS, BLOCKS), 1)
    held = jnp.where(jnp.broadcast_to(owner_of[...], (BLOCKS, BLOCKS)) == slot, block, 0)
    by_owner_v[...] = jnp.max(held.T, axis=0, keepdims=True)
    to_smem = pltpu.make_async_copy(by_owner_v, by_owner, load_sem.at[5])
    to_smem.start()
    to_smem.wait()
    load_grad.wait()
    for load in loads:
        load.start()

    @pl.when(r == 0)
    def _():
        pl.semaphore_wait(barrier, CHIPS - 1)

    @pl.when(r == 1)
    def _():
        pl.semaphore_wait(barrier, CHIPS + 1)

    def swap(c):
        part = pl.ds(c * CHUNK, CHUNK)
        return pltpu.make_async_remote_copy(
            stage.at[part], partner_part.at[part], swap_send.at[c], swap_recv.at[c],
            device_id=(f, other), device_id_type=MESH,
        )

    def target(p, core):
        return partner_chip(f, 2 * lax.rem(p, CHIPS // 2) + core), lax.div(p, CHIPS // 2)

    @pl.loop(0, CHIPS // CHUNK)
    def _(c):
        @pl.loop(0, CHUNK)
        def _(j):
            p = c * CHUNK + j
            to, core = target(p, other)
            stage[p] = grad[by_owner[0, 2 * to + core]]

        swap(c).start()

    @pl.loop(0, CHIPS // CHUNK)
    def _(c):
        swap(c).wait_recv()

        @pl.loop(0, CHUNK)
        def _(j):
            p = c * CHUNK + j
            to, core = target(p, r)
            mine = grad[by_owner[0, 2 * to + core]].astype(F32)
            summed[p] = (mine + partner_part[p].astype(F32)).astype(BF16)

            @pl.when(p + r > 0)
            def _():
                pltpu.make_async_remote_copy(
                    summed.at[p], gathered.at[f], fwd_send.at[core], fwd_recv,
                    device_id=(to, core), device_id_type=MESH,
                ).start()

    @pl.when(r == 0)
    def _():
        gathered[f] = summed[0]

    for load in loads:
        load.wait()

    @pl.loop(0, CHIPS)
    def _(i):
        lperm[i] = lroot[pl.ds(pl.multiple_of(partner_chip(f, i) * ROWS, ROWS), ROWS), :]

    rest = pl.ds(0, CHIPS - 1)

    @pl.when(r == 0)
    def _():
        pltpu.make_async_copy(gathered.at[rest], gathered.at[rest], fwd_recv).wait()

    @pl.when(r == 1)
    def _():
        pltpu.make_async_copy(gathered, gathered, fwd_recv).wait()

    @pl.loop(0, CHIPS // LGR_CHUNK)
    def _(c):
        part = lperm[pl.ds(c * LGR_CHUNK, LGR_CHUNK)].reshape(LGR_CHUNK * ROWS, BS)
        whole = gathered[...].reshape(BS, BS)
        applied = jnp.dot(part, whole, preferred_element_type=F32).astype(BF16)
        done = jnp.dot(applied, rroot[...], preferred_element_type=F32)
        outgoing[pl.ds(c * 2 * LGR_CHUNK, 2 * LGR_CHUNK)] = done.reshape(2 * LGR_CHUNK, HALF, BS).astype(BF16)

        @pl.loop(0, 2 * LGR_CHUNK)
        def _(j):
            h = c * 2 * LGR_CHUNK + j
            to = partner_chip(f, lax.div(h, 2))
            core = lax.rem(h, 2)

            @pl.when(2 * to + core != me)
            def _():
                pltpu.make_async_remote_copy(
                    outgoing.at[h], returned.at[me], back_send, back_recv,
                    device_id=(to, core), device_id_type=MESH,
                ).start()

    returned[me] = outgoing[r]

    @pl.loop(0, 4)
    def _(c):
        rows = pl.ds(pl.multiple_of(c * 256, 256), 256)
        whole = gathered[...].reshape(BS, BS)
        part = gathered[pl.ds(c * 16, 16)].reshape(256, BS)
        gram = lax.dot_general(part, whole, (((1,), (1,)), ((), ())), preferred_element_type=F32)
        new_left[0, rows, :] += gram * (1.0 / BS)

    @pl.loop(0, 4)
    def _(c):
        rows = pl.ds(pl.multiple_of(c * 256, 256), 256)
        whole = gathered[...].reshape(BS, BS)
        part = gathered[:, :, rows].reshape(BS, 256)
        gram = lax.dot_general(part, whole, (((0,), (0,)), ((), ())), preferred_element_type=F32)
        new_right[0, rows, :] += gram * (1.0 / BS)

    @pl.loop(0, CHIPS // CHUNK)
    def _(c):
        swap(c).wait_send()

    half = pl.ds(0, CHIPS // 2)
    half_less = pl.ds(0, CHIPS // 2 - 1)

    @pl.when(r == 0)
    def _():
        pltpu.make_async_copy(summed.at[half_less], summed.at[half_less], fwd_send.at[0]).wait()

    @pl.when(r == 1)
    def _():
        pltpu.make_async_copy(summed.at[half], summed.at[half], fwd_send.at[0]).wait()

    pltpu.make_async_copy(summed.at[half], summed.at[half], fwd_send.at[1]).wait()
    all_but_me = pl.ds(0, BLOCKS - 1)
    pltpu.make_async_copy(returned.at[all_but_me], returned.at[all_but_me], back_send).wait()
    pltpu.make_async_copy(returned.at[all_but_me], returned.at[all_but_me], back_recv).wait()


def write_out(owner_of, left, right, returned, new_left, new_right, direction, sem):
    writes = [
        pltpu.make_async_copy(left, new_left, sem.at[0]),
        pltpu.make_async_copy(right, new_right, sem.at[1]),
    ]
    for write in writes:
        write.start()

    @pl.loop(0, BLOCKS)
    def _(b):
        pltpu.make_async_copy(returned.at[owner_of[b]], direction.at[b], sem.at[2]).start()

    for write in writes:
        write.wait()
    pltpu.make_async_copy(returned, direction, sem.at[2]).wait()


def body(grad_parts, owner_of, left_stats, right_stats, left_root, right_root):
    anywhere = pl.BlockSpec(memory_space=pl.ANY)
    vmem = pl.BlockSpec(memory_space=pltpu.VMEM)
    smem = pl.BlockSpec(memory_space=pltpu.SMEM)
    left, right, returned = pl.pallas_call(
        kernel,
        out_shape=(
            pltpu.VMEM((1, BS, BS), F32),
            pltpu.VMEM((1, BS, BS), F32),
            pltpu.VMEM((BLOCKS, HALF, BS), BF16),
        ),
        in_specs=[anywhere] * 6,
        out_specs=(vmem, vmem, vmem),
        scratch_shapes=[
            pltpu.VMEM((BLOCKS, ROWS, BS), BF16),
            pltpu.VMEM((CHIPS, ROWS, BS), BF16),
            pltpu.VMEM((CHIPS, ROWS, BS), BF16),
            pltpu.VMEM((CHIPS, ROWS, BS), BF16),
            pltpu.VMEM((CHIPS, ROWS, BS), BF16),
            pltpu.VMEM((BS, BS), BF16),
            pltpu.VMEM((CHIPS, ROWS, BS), BF16),
            pltpu.VMEM((BS, BS), BF16),
            pltpu.VMEM((BLOCKS, HALF, BS), BF16),
            pltpu.VMEM((1, BLOCKS), jnp.int32),
            pltpu.VMEM((1, BLOCKS), jnp.int32),
            pltpu.SMEM((1, BLOCKS), jnp.int32),
            pltpu.SemaphoreType.DMA((7,)),
            pltpu.SemaphoreType.DMA((CHIPS // CHUNK,)),
            pltpu.SemaphoreType.DMA((CHIPS // CHUNK,)),
            pltpu.SemaphoreType.DMA((2,)),
            pltpu.SemaphoreType.DMA,
            pltpu.SemaphoreType.DMA,
            pltpu.SemaphoreType.DMA,
        ],
        compiler_params=pltpu.CompilerParams(
            collective_id=0, has_side_effects=True, vmem_limit_bytes=52 * 2**20
        ),
        cost_estimate=pl.CostEstimate(
            flops=8 * BS**3, bytes_accessed=16 * 2**20, transcendentals=0
        ),
        name="shampoo_step",
    )(owner_of[None], grad_parts, left_stats, right_stats, left_root, right_root)
    return pl.pallas_call(
        write_out,
        out_shape=(
            jax.ShapeDtypeStruct((1, BS, BS), F32),
            jax.ShapeDtypeStruct((1, BS, BS), F32),
            jax.ShapeDtypeStruct((BLOCKS, HALF, BS), BF16),
        ),
        in_specs=[smem] + [anywhere] * 3,
        out_specs=(anywhere, anywhere, anywhere),
        scratch_shapes=[pltpu.SemaphoreType.DMA((3,))],
        compiler_params=pltpu.CompilerParams(vmem_limit_bytes=2 * 2**20),
        name="write_out",
    )(owner_of, left, right, returned)


def solution(mesh):
    placed = (
        P("rep", None, "fsdp", None),
        P(),
        P(("fsdp", "rep"), None, None),
        P(("fsdp", "rep"), None, None),
        P(("fsdp", "rep"), None, None),
        P(("fsdp", "rep"), None, None),
    )
    return jax.shard_map(
        body,
        mesh=mesh,
        in_specs=placed,
        out_specs=(
            P(("fsdp", "rep"), None, None),
            P(("fsdp", "rep"), None, None),
            P(None, ("fsdp", "rep"), None),
        ),
        check_vma=False,
    )
```
